512 devices in a mesh: dp: 16 (over x, z_lo, core), ctx: 32 (over z_hi, y).
Axes of the slice: x: 4, y: 8, z: 8 (z_hi: 4, z_lo: 2; z = z_hi * 2 + z_lo), core: 2. Of those that a mesh axis runs over, the one named last changes fastest.
Arguments:
- queries: bfloat16 [16, 4096, 1024], P('dp', 'ctx'), may hold values from -60 to 60
- keys: bfloat16 [16, 4096, 128], P('dp', 'ctx'), may hold values from -6 to 6
- values: bfloat16 [16, 4096, 192], P('dp', 'ctx'), may hold values from -96 to 96
- features_fine: bfloat16 [16, 8192, 1536], P('dp', 'ctx'), may hold values from -6 to 6
- rc_state: bfloat16 [16, 4096, 1536], P('dp', 'ctx'), may hold values from -6 to 6
- conv_weight: float32 [5, 1536], replicated, may hold values from -2.5 to 2.5
Outputs:
- d_fine: bfloat16 [16, 8192, 1536], P('dp', 'ctx')
- d_weight: float32 [5, 1536], replicated
The draws below stay inside these ranges and needn't reach their ends.
All inputs are finite; a program needn't handle non-finite values.
Results may differ from the reference program's by a relative error of at most 0.0085.
Values may be sent and summed in bfloat16 or wider, within the bound.
A program may use at most 64 MiB of HBM per device.

```python
import math
import jax
import jax.numpy as jnp
from jax import lax

D = 1536
HEADS = 8
DK = 128
DV = 192
KW = 5
LEN = 4096
XLEN = 8192
SEQS = 16


def shared_keys(key):
    sub = jax.random.fold_in(key, 11)
    base = jnp.clip(jax.random.normal(sub, (SEQS, LEN, DK), jnp.float32), -6.0, 6.0)
    return base


def draw_keys(key, part):
    return shared_keys(key).astype(jnp.bfloat16)


def draw_queries(key, part):
    sub = jax.random.fold_in(key, 12)
    out = jnp.clip(jax.random.normal(sub, (SEQS, LEN, HEADS, DK), jnp.float32), -6.0, 6.0)
    return out.reshape(SEQS, LEN, HEADS * DK).astype(jnp.bfloat16)


def shard_levels(rng, dims, pieces, low, top_value):
    gain = 1.0
    for axis_at, blocks in pieces:
        heights = jax.random.uniform(jax.random.fold_in(jax.random.fold_in(rng, 6), axis_at), (blocks,), jnp.float32, low / len(pieces), top_value / len(pieces))
        gain = gain * jnp.repeat(jnp.exp(heights), dims[axis_at] // blocks).reshape((-1,) + (1,) * (len(dims) - 1 - axis_at))
    return gain


def bell_draw(stream_key, shape, spread, limit, shards=(), held_as=jnp.bfloat16):
    drawn = jax.random.normal(stream_key, shape, jnp.float32) * spread
    if len(shards) > 0:
        drawn = shard_levels(stream_key, shape, shards, -0.22, 0.18) * drawn
    return jnp.clip(drawn, min=-limit, max=limit).astype(held_as)


def setup_inputs(seed: int = 0) -> dict:
    key_of = jax.random.split(jax.random.key(seed), 7)
    return {
        "queries": draw_queries(jax.random.fold_in(key_of[6], 71), 0),
        "keys": draw_keys(jax.random.fold_in(key_of[6], 71), 0),
        "values": bell_draw(key_of[2], (SEQS, LEN, DV), 16.0, 96.0, ((0, 16), (1, 32))),
        "features_fine": bell_draw(key_of[3], (SEQS, XLEN, D), 1.0, 6.0, ((0, 16), (1, 32))),
        "rc_state": bell_draw(key_of[4], (SEQS, LEN, D), 1.0, 6.0, ((0, 16), (1, 32))),
        "conv_weight": bell_draw(key_of[5], (KW, D), KW ** -0.5, 2.5, (), jnp.float32),
    }


def attend_block(block, keys_f, values_f):
    rows = block.shape[0]
    q_f = block.astype(jnp.float32).reshape(rows, HEADS, DK)
    scores = jnp.einsum('qhd,kd->qhk', q_f, keys_f) * DK ** (-0.5)
    top = lax.optimization_barrier(jnp.max(scores, axis=-1, keepdims=True))
    expd = jnp.exp(scores - top)
    total = lax.optimization_barrier(jnp.sum(expd, axis=-1))
    weights = expd.astype(jnp.bfloat16).astype(jnp.float32)
    out = jnp.einsum('qhk,kv->qhv', weights, values_f) / total[..., None]
    return out.reshape(rows, HEADS * DV)

def attend_seq(items):
    q_seq, k_seq, v_seq = items
    keys_f = k_seq.astype(jnp.float32)
    values_f = v_seq.astype(jnp.float32)
    block = math.gcd(LEN, 512)
    blocks = q_seq.reshape(LEN // block, block, HEADS * DK)
    out = lax.map(lambda b: attend_block(b, keys_f, values_f), blocks)
    return out.reshape(LEN, HEADS * DV)

def reference(queries, keys, values, features_fine, rc_state, conv_weight):
    attended = lax.map(attend_seq, (queries, keys, values))
    fine = features_fine.astype(jnp.float32)
    padded = jnp.pad(fine, ((0, 0), (2, 2), (0, 0)))
    taps = [padded[:, k:k + 2 * LEN:2, :] for k in range(KW)]
    coarse = jnp.zeros((SEQS, LEN, D), jnp.float32)
    for k in range(KW):
        coarse = coarse + conv_weight[k] * taps[k]
    grad = coarse + attended - rc_state[:, ::-1, :].astype(jnp.float32)
    gpad = jnp.pad(grad, ((0, 0), (1, 1), (0, 0)))
    even = conv_weight[0] * gpad[:, 2:] + conv_weight[2] * gpad[:, 1:-1] + conv_weight[4] * gpad[:, :-2]
    odd = conv_weight[1] * gpad[:, 2:] + conv_weight[3] * gpad[:, 1:-1]
    d_fine = jnp.stack([even, odd], axis=2).reshape(SEQS, XLEN, D).astype(jnp.bfloat16)
    scale = 1.0 / math.sqrt(SEQS * LEN)
    d_weight = jnp.stack([lax.optimization_barrier(jnp.sum(grad * taps[k], axis=(0, 1))) for k in range(KW)]) * scale
    return (d_fine, d_weight)
```

```python
import functools
import heapq
import math

import jax
import jax.numpy as jnp
from jax import lax
from jax.experimental import pallas as pl
from jax.experimental.pallas import tpu as pltpu
from jax.sharding import PartitionSpec as P

HEADS = 8
DK = 128
DV = 192
VROWS = DV
ROWS = 128
D = HEADS * DV
KW = 5
NA, NY = 4, 8
MESH = pl.DeviceIdType.MESH
F32 = jnp.float32
BF16 = jnp.bfloat16


def block_sends():
    sends = {}
    for da in range(NA):
        cw = 4 - da % 2
        for dy in range(NY):
            behind = (NY - dy) % NY
            v, k = [], []
            if dy == 0:
                if da == 0:
                    v += [("a+", ("V", 3, 0)), ("a-", ("V", 1, 0)), ("a2", ("V", 2, 0))]
                v += [("y+", ("V", da, 7)), ("y-", ("V", da, 1))]
            elif behind <= cw:
                if behind < cw:
                    v.append(("y+", ("V", da, dy - 1)))
            elif dy < 7 - cw:
                v.append(("y-", ("V", da, dy + 1)))
            sends[("V", da, dy)] = v
            if da == 0:
                if dy == 0:
                    k += [("y+", ("K", 0, 7)), ("y-", ("K", 0, 1))]
                elif behind < 4:
                    k.append(("y+", ("K", 0, dy - 1)))
                elif dy < 3:
                    k.append(("y-", ("K", 0, dy + 1)))
                k += [("a+", ("K", 3, dy)), ("a-", ("K", 1, dy))]
            elif da == 3 and dy % 2 == 0:
                k.append(("a+", ("K", 2, dy)))
            elif da == 1 and dy % 2 == 1:
                k.append(("a-", ("K", 2, dy)))
            sends[("K", da, dy)] = k
    return sends


def arrival_order(sends):
    free = {"y+": 0.0, "y-": 0.0, "a+": 0.0, "a-": 0.0}
    cost = {"V": 1.06, "K": 0.71}
    queue = [(0.0, 0, ("K", 0, 0)), (0.0, 1, ("V", 0, 0))]
    order, n = [], 2
    while queue:
        now, _, key = heapq.heappop(queue)
        order.append(key)
        for link, child in sends[key]:
            if link == "a2":
                end = max(now, free["a+"], free["a-"]) + 2 * cost[key[0]]
                free["a+"] = free["a-"] = end
                late = 3.6
            else:
                along_y = link[0] == "y"
                end = max(now, free[link]) + cost[key[0]] * (1 if along_y else 2)
                free[link] = end
                late = 1.8 if along_y else 2.4
            heapq.heappush(queue, (end + late, n, child))
            n += 1
    return order


def kernel(
    q_ref, k_ref, v_ref, ff_ref, rc_ref, w_ref, df_ref, dw_ref,
    kbuf, vbuf, rcin, qs, vx, top, acc, wide, base, ev, od, grd, halo_out, halo_in, edge_out, edge_in,
    send_sem, k_sem, v_sem, m_send, m_recv, h_send, h_recv, e_send, e_recv,
):
    dp, ctx = lax.axis_index("dp"), lax.axis_index("ctx")
    a, y = ctx // NY, lax.rem(ctx, NY)
    count = NA * NY

    def at(a_new, y_new):
        return (dp, lax.rem(a_new, NA) * NY + lax.rem(y_new, NY))

    right, left = (dp, lax.rem(ctx + 1, count)), (dp, lax.rem(ctx + count - 1, count))
    mirror = (dp, count - 1 - ctx)
    peers = {
        "y+": at(a, y + 1), "y-": at(a, y + NY - 1), "a+": at(a + 1, y), "a-": at(a + NA - 1, y), "a2": at(a + 2, y),
    }
    barrier = pltpu.get_barrier_semaphore()
    greeted = list(peers.values()) + [right, left, mirror]
    for peer in greeted:
        pl.semaphore_signal(barrier, inc=1, device_id=peer, device_id_type=MESH)

    kbuf[y, a] = k_ref[...]
    v_own = v_ref[...]
    tail = v_own[:, 128:]
    vbuf[y, a, 0:ROWS, :] = v_own[:, :128]
    vbuf[y, a, ROWS:VROWS, :] = jnp.concatenate([tail[:64], tail[64:]], axis=1)

    def widen(i, _):
        cols = pl.ds(pl.multiple_of(i * 128, 128), 128)
        wide[i] = ff_ref[:, cols].astype(F32)
        return 0

    lax.fori_loop(0, D // 128, widen, 0)
    halo_out[0] = ff_ref[2 * ROWS - 16 : 2 * ROWS, :].astype(F32)[14:16]
    halo_out[1] = ff_ref[0:16, :].astype(F32)[0:2]
    pl.semaphore_wait(barrier, len(greeted))

    halo = [
        pltpu.make_async_remote_copy(
            halo_out.at[i], halo_in.at[i], h_send.at[i], h_recv.at[i], device_id=peer, device_id_type=MESH
        )
        for i, peer in enumerate((right, left))
    ]
    mirrored = pltpu.make_async_remote_copy(rc_ref, rcin, m_send, m_recv, device_id=mirror, device_id_type=MESH)

    sends = block_sends()
    order = arrival_order(sends)
    started = []

    def block(key):
        o_a, o_y = lax.rem(a + key[1], NA), lax.rem(y + key[2], NY)
        buf, sem = (kbuf, k_sem) if key[0] == "K" else (vbuf, v_sem)
        return buf.at[o_y, o_a], sem.at[o_y, o_a]

    def event(key):
        ref, sem = block(key)
        if key[1:] != (0, 0):
            pltpu.make_async_remote_copy(
                ref, ref, sem, sem, device_id=peers["y+"], device_id_type=MESH
            ).wait_recv()
        for link, _ in sends[key]:
            copy = pltpu.make_async_remote_copy(
                ref, ref, send_sem.at[len(started)], sem, device_id=peers[link], device_id_type=MESH
            )
            copy.start()
            started.append(copy)

    def prepare():
        def heads(h, _):
            qs[h] = q_ref[:, pl.ds(pl.multiple_of(h * DK, DK), DK)]
            top[h] = jnp.full((ROWS, 128), -1e30, F32)
            acc[h] = jnp.zeros((ROWS, 256), F32)
            return 0

        lax.fori_loop(0, HEADS, heads, 0)
        lane = lax.broadcasted_iota(jnp.int32, (NA * ROWS, 128), 1)
        vx[:, 128:256] = jnp.where(lane < 64, 0.0, 1.0).astype(BF16)

    def gather_values(dy):
        o_y = lax.rem(y + dy, NY)
        for i in range(NA):
            vx[i * ROWS : (i + 1) * ROWS, 0:128] = vbuf[o_y, i, 0:ROWS, :]
            packed = vbuf[o_y, i, ROWS:VROWS, :]
            vx[i * ROWS : i * ROWS + 64, 128:192] = packed[:, :64]
            vx[i * ROWS + 64 : (i + 1) * ROWS, 128:192] = packed[:, 64:]

    factor = DK ** (-0.5) * math.log2(math.e)

    def attend(dy, low, high):
        o_y = lax.rem(y + dy, NY)

        def head(h, _):
            keys = kbuf[o_y].reshape(NA * ROWS, DK)
            s = lax.dot_general(qs[h], keys, (((1,), (1,)), ((), ())), preferred_element_type=F32)
            old = top[h]
            new = jnp.maximum(old, jnp.max(s, axis=1, keepdims=True))
            p = jnp.exp2((s - new[:, :1]) * factor).astype(BF16)
            fade = jnp.exp2((old - new) * factor)
            fade = jnp.concatenate([fade, fade], axis=1)
            acc[h] = acc[h] * fade + jnp.dot(p, vx[...], preferred_element_type=F32)
            top[h] = new
            return 0

        lax.fori_loop(low, high, head, 0)

    def convolve():
        for copy in halo:
            copy.wait_recv()
        inner_left = jnp.where(ctx > 0, 1.0, 0.0)
        inner_right = jnp.where(ctx < count - 1, 1.0, 0.0)
        ev[7:8, :] = halo_in[0, 0:1, :] * inner_left
        od[7:8, :] = halo_in[0, 1:2, :] * inner_left
        ev[136:137, :] = halo_in[1, 0:1, :] * inner_right

        def chunk(i, _):
            cols = pl.ds(pl.multiple_of(i * 128, 128), 128)
            ev[8:136, cols] = wide[i, pl.ds(0, ROWS, stride=2), :]
            od[8:136, cols] = wide[i, pl.ds(1, ROWS, stride=2), :]
            w = w_ref[:, cols]
            base[:, cols] = (
                w[0:1] * ev[7:135, cols]
                + w[1:2] * od[7:135, cols]
                + w[2:3] * ev[8:136, cols]
                + w[3:4] * od[8:136, cols]
                + w[4:5] * ev[9:137, cols]
            )
            return 0

        lax.fori_loop(0, D // 128, chunk, 0)

    ready, done = [], {}
    for n, key in enumerate(order):
        event(key)
        if n == 1:
            for copy in halo:
                copy.start()
            mirrored.start()
            prepare()
        if n == 9:
            convolve()
        done[key[2]] = done.get(key[2], 0) + 1
        if done[key[2]] == 2 * NA:
            ready += [(key[2], h) for h in range(0, HEADS, 2)]
        if n < len(order) - 1 and ready:
            dy, h = ready.pop(0)
            if h == 0:
                gather_values(dy)
            attend(dy, h, h + 2)
    while ready:
        dy, h = ready[0]
        if h == 0:
            gather_values(dy)
        attend(dy, h, HEADS)
        ready = [r for r in ready if r[0] != dy]

    mirrored.wait_recv()
    row = lax.broadcasted_iota(jnp.int32, (ROWS, ROWS), 0)
    col = lax.broadcasted_iota(jnp.int32, (ROWS, ROWS), 1)
    turn = jnp.where(row + col == ROWS - 1, 1.0, 0.0).astype(BF16)

    def finish(j, _):
        cols = pl.ds(pl.multiple_of(j * 2 * DV, 128), 2 * DV)
        one, two = acc[2 * j], acc[2 * j + 1]
        attended = jnp.concatenate(
            [one[:, :DV] / one[:, DV : DV + 1], two[:, :DV] / two[:, DV : DV + 1]], axis=1
        )
        grd[8:136, cols] = base[:, cols] + attended - jnp.dot(turn, rcin[:, cols], preferred_element_type=F32)
        return 0

    lax.fori_loop(0, HEADS // 2, finish, 0)
    edge_out[0] = grd[135:136, :]
    edge_out[1] = grd[8:9, :]
    edges = [
        pltpu.make_async_remote_copy(
            edge_out.at[i], edge_in.at[i], e_send.at[i], e_recv.at[i], device_id=peer, device_id_type=MESH
        )
        for i, peer in enumerate((right, left))
    ]
    for copy in edges:
        copy.start()

    def weigh(i, _):
        cols = pl.ds(pl.multiple_of(i * 128, 128), 128)
        g = grd[8:136, cols]
        taps = (ev[7:135, cols], od[7:135, cols], ev[8:136, cols], od[8:136, cols], ev[9:137, cols])
        dw_ref[:, cols] = jnp.concatenate([jnp.sum(g * tap, axis=0, keepdims=True) for tap in taps], axis=0)
        return 0

    lax.fori_loop(0, D // 128, weigh, 0)
    for copy in edges:
        copy.wait_recv()
    grd[7:8, :] = edge_in[0] * jnp.where(ctx > 0, 1.0, 0.0)
    grd[136:137, :] = edge_in[1] * jnp.where(ctx < count - 1, 1.0, 0.0)

    def spread(i, _):
        cols = pl.ds(pl.multiple_of(i * 128, 128), 128)
        w = w_ref[:, cols]
        before, here, after = grd[7:135, cols], grd[8:136, cols], grd[9:137, cols]
        wide[i, pl.ds(0, ROWS, stride=2), :] = w[0:1] * after + w[2:3] * here + w[4:5] * before
        wide[i, pl.ds(1, ROWS, stride=2), :] = w[1:2] * after + w[3:4] * here
        df_ref[:, cols] = wide[i].astype(BF16)
        return 0

    lax.fori_loop(0, D // 128, spread, 0)
    for copy in started + halo + edges + [mirrored]:
        copy.wait_send()


def run(queries, keys, values, features_fine, rc_state, conv_weight):
    vmem = pl.BlockSpec(memory_space=pltpu.VMEM)
    dma = pltpu.SemaphoreType.DMA
    n_sends = sum(len(s) for s in block_sends().values())
    return pl.pallas_call(
        kernel,
        name="attend_and_convolve",
        out_shape=(jax.ShapeDtypeStruct((2 * ROWS, D), BF16), jax.ShapeDtypeStruct((KW, D), F32)),
        in_specs=[vmem] * 6,
        out_specs=(vmem, vmem),
        scratch_shapes=[
            pltpu.VMEM((NY, NA, ROWS, DK), BF16),
            pltpu.VMEM((NY, NA, VROWS, 128), BF16),
            pltpu.VMEM((ROWS, D), BF16),
            pltpu.VMEM((HEADS, ROWS, DK), BF16),
            pltpu.VMEM((NA * ROWS, 256), BF16),
            pltpu.VMEM((HEADS, ROWS, 128), F32),
            pltpu.VMEM((HEADS, ROWS, 256), F32),
            pltpu.VMEM((D // 128, 2 * ROWS, 128), F32),
            pltpu.VMEM((ROWS, D), F32),
            pltpu.VMEM((ROWS + 16, D), F32),
            pltpu.VMEM((ROWS + 16, D), F32),
            pltpu.VMEM((ROWS + 16, D), F32),
            pltpu.VMEM((2, 2, D), F32),
            pltpu.VMEM((2, 2, D), F32),
            pltpu.VMEM((2, 1, D), F32),
            pltpu.VMEM((2, 1, D), F32),
            dma((n_sends,)),
            dma((NY, NA)),
            dma((NY, NA)),
            dma,
            dma,
            dma((2,)),
            dma((2,)),
            dma((2,)),
            dma((2,)),
        ],
        compiler_params=pltpu.CompilerParams(
            collective_id=0, has_side_effects=True, vmem_limit_bytes=40 * 2**20
        ),
        cost_estimate=pl.CostEstimate(flops=2_700_000_000, bytes_accessed=4_000_000, transcendentals=4_200_000),
    )(queries, keys, values, features_fine, rc_state, conv_weight)


def body(queries, keys, values, features_fine, rc_state, conv_weight):
    d_fine, partial = run(queries[0], keys[0], values[0], features_fine[0], rc_state[0], conv_weight)
    summed = lax.psum(partial, ("dp", "ctx"))
    scale = 1.0 / math.sqrt(lax.axis_size("dp") * lax.axis_size("ctx") * ROWS)
    return d_fine[None], summed * scale


def solution(mesh):
    split = P("dp", "ctx", None)
    return jax.shard_map(
        body, mesh=mesh, in_specs=(split,) * 5 + (P(),), out_specs=(split, P()), check_vma=False
    )
```

```python
import heapq
import math

import jax
import jax.numpy as jnp
from jax import lax
from jax.experimental import pallas as pl
from jax.experimental.pallas import tpu as pltpu
from jax.sharding import PartitionSpec as P

HEADS = 8
DK = 128
DV = 192
ROWS = 128
D = HEADS * DV
KW = 5
NA, NY = 4, 8
NX, NZ = 4, 8
MESH = pl.DeviceIdType.MESH
F32 = jnp.float32
BF16 = jnp.bfloat16


def block_sends():
    sends = {}
    for da in range(NA):
        cw = 4 - da % 2
        for dy in range(NY):
            behind = (NY - dy) % NY
            v, k = [], []
            if dy == 0:
                if da == 0:
                    v += [("a+", ("V", 3, 0)), ("a-", ("V", 1, 0)), ("a2", ("V", 2, 0))]
                v += [("y+", ("V", da, 7)), ("y-", ("V", da, 1))]
            elif behind <= cw:
                if behind < cw:
                    v.append(("y+", ("V", da, dy - 1)))
            elif dy < 7 - cw:
                v.append(("y-", ("V", da, dy + 1)))
            sends[("V", da, dy)] = v
            if da == 0:
                if dy == 0:
                    k += [("y+", ("K", 0, 7)), ("y-", ("K", 0, 1))]
                elif behind < 4:
                    k.append(("y+", ("K", 0, dy - 1)))
                elif dy < 3:
                    k.append(("y-", ("K", 0, dy + 1)))
                k += [("a+", ("K", 3, dy)), ("a-", ("K", 1, dy))]
            elif da == 3 and dy % 2 == 0:
                k.append(("a+", ("K", 2, dy)))
            elif da == 1 and dy % 2 == 1:
                k.append(("a-", ("K", 2, dy)))
            sends[("K", da, dy)] = k
    return sends


def arrival_order(sends):
    free = {"y+": 0.0, "y-": 0.0, "a+": 0.0, "a-": 0.0}
    cost = {"V": 1.06, "K": 0.71}
    queue = [(0.0, 0, ("K", 0, 0)), (0.0, 1, ("V", 0, 0))]
    order, n = [], 2
    while queue:
        now, _, key = heapq.heappop(queue)
        order.append(key)
        for link, child in sends[key]:
            if link == "a2":
                end = max(now, free["a+"], free["a-"]) + 2 * cost[key[0]]
                free["a+"] = free["a-"] = end
                late = 3.6
            else:
                along_y = link[0] == "y"
                end = max(now, free[link]) + cost[key[0]] * (1 if along_y else 2)
                free[link] = end
                late = 1.8 if along_y else 2.4
            heapq.heappush(queue, (end + late, n, child))
            n += 1
    return order


def kernel(
    q_ref, k_ref, v_ref, ff_ref, rc_ref, w_ref, df_ref, dw_ref,
    kbuf, vbuf, rcin, qs, kx, vx, top, acc, fine, wide, base, ev, od, grd, halo_out, halo_in, edge_out, edge_in,
    part, core_in, x_in, z_in, y_in, final,
    local, send_sem, k_sem, v_sem, m_recv, h_recv, e_recv, c_recv, x_recv, z_recv, y_recv,
):
    dp, ctx = lax.axis_index("dp"), lax.axis_index("ctx")
    a, y = ctx // NY, lax.rem(ctx, NY)
    core, zlo, x = lax.rem(dp, 2), lax.rem(dp // 2, 2), dp // 4
    z = a * 2 + zlo
    count = NA * NY

    def at(a_new, y_new):
        return (dp, lax.rem(a_new, NA) * NY + lax.rem(y_new, NY))

    right, left = (dp, lax.rem(ctx + 1, count)), (dp, lax.rem(ctx + count - 1, count))
    mirror = (dp, count - 1 - ctx)
    peers = {
        "y+": at(a, y + 1), "y-": at(a, y + NY - 1), "a+": at(a + 1, y), "a-": at(a + NA - 1, y), "a2": at(a + 2, y),
    }
    other_core = (dp + 1 - 2 * core, ctx)
    x_peers = [(lax.rem(x + i, NX) * 4 + zlo * 2 + core, ctx) for i in range(1, NX)]
    z_peers = []
    for i in range(1, NZ):
        z_new = lax.rem(z + i, NZ)
        z_peers.append((x * 4 + lax.rem(z_new, 2) * 2 + core, z_new // 2 * NY + y))
    y_peers = [at(a, y + i) for i in range(1, NY)]
    barrier = pltpu.get_barrier_semaphore()
    greeted = [right, left, mirror, other_core] + x_peers + z_peers + y_peers
    for peer in greeted:
        pl.semaphore_signal(barrier, inc=1, device_id=peer, device_id_type=MESH)

    own_k = pltpu.make_async_copy(k_ref, kbuf.at[y, a], local.at[0])
    own_v = pltpu.make_async_copy(v_ref, vbuf.at[y, a, pl.ds(0, DV)], local.at[1])
    own_f = pltpu.make_async_copy(ff_ref, fine, local.at[2])
    own_q = [
        pltpu.make_async_copy(q_ref.at[:, pl.ds(h * DK, DK)], qs.at[h], local.at[3 + h]) for h in range(HEADS)
    ]
    for copy in [own_f, own_k, own_v] + own_q:
        copy.start()

    started = []

    def push(src, dst, recv_sem, peer):
        copy = pltpu.make_async_remote_copy(
            src, dst, send_sem.at[len(started)], recv_sem, device_id=peer, device_id_type=MESH
        )
        copy.start()
        started.append(copy)

    def landed(ref, sem):
        pltpu.make_async_remote_copy(ref, ref, sem, sem, device_id=other_core, device_id_type=MESH).wait_recv()

    sends = block_sends()
    order = arrival_order(sends)

    def event(key):
        o_a, o_y = lax.rem(a + key[1], NA), lax.rem(y + key[2], NY)
        if key[0] == "K":
            ref, sem = kbuf.at[o_y, o_a], k_sem.at[o_y, o_a]
        else:
            ref, sem = vbuf.at[o_y, o_a, pl.ds(0, DV)], v_sem.at[o_y, o_a]
        if key[1:] != (0, 0):
            landed(ref, sem)
        for link, _ in sends[key]:
            push(ref, ref, sem, peers[link])

    def prepare():
        def heads(h, _):
            top[h] = jnp.full((ROWS, 128), -1e30, F32)
            acc[h] = jnp.zeros((ROWS, 256), F32)
            return 0

        lax.fori_loop(0, HEADS, heads, 0)
        vx[:, DV:256] = jnp.ones((NA * ROWS, 64), BF16)

    def gather_keys(dy):
        o_y = lax.rem(y + dy, NY)
        for i in range(NA):
            rows = slice(i * ROWS, (i + 1) * ROWS)
            kx[:, rows] = kbuf[o_y, i].T
            vx[rows, 0:128] = vbuf[o_y, i, 0:128, :].T
            vx[rows, 128:192] = vbuf[o_y, i, 128:192, :].T

    factor = DK ** (-0.5) * math.log2(math.e)

    def attend(low, high):
        def head(h, _):
            s = jnp.dot(qs[h], kx[...], preferred_element_type=F32)
            old = top[h]
            new = jnp.maximum(old, jnp.max(s, axis=1, keepdims=True))
            p = jnp.exp2((s - new[:, :1]) * factor).astype(BF16)
            fade = jnp.exp2((old - new) * factor)
            fade = jnp.concatenate([fade, fade], axis=1)
            acc[h] = acc[h] * fade + jnp.dot(p, vx[...], preferred_element_type=F32)
            top[h] = new
            return 0

        lax.fori_loop(low, high, head, 0)

    def convolve():
        landed(halo_in.at[0], h_recv.at[0])
        landed(halo_in.at[1], h_recv.at[1])
        inner_left = jnp.where(ctx > 0, 1.0, 0.0)
        inner_right = jnp.where(ctx < count - 1, 1.0, 0.0)
        ev[7:8, :] = halo_in[0, 0:1, :] * inner_left
        od[7:8, :] = halo_in[0, 1:2, :] * inner_left
        ev[136:137, :] = halo_in[1, 0:1, :] * inner_right

        def chunk(i, _):
            cols = pl.ds(pl.multiple_of(i * 128, 128), 128)
            wide[i] = fine[:, cols].astype(F32)
            ev[8:136, cols] = wide[i, pl.ds(0, ROWS, stride=2), :]
            od[8:136, cols] = wide[i, pl.ds(1, ROWS, stride=2), :]
            w = w_ref[:, cols]
            base[:, cols] = (
                w[0:1] * ev[7:135, cols]
                + w[1:2] * od[7:135, cols]
                + w[2:3] * ev[8:136, cols]
                + w[3:4] * od[8:136, cols]
                + w[4:5] * ev[9:137, cols]
            )
            return 0

        lax.fori_loop(0, D // 128, chunk, 0)

    own_f.wait()
    halo_out[0] = fine[2 * ROWS - 16 : 2 * ROWS, :].astype(F32)[14:16]
    halo_out[1] = fine[0:16, :].astype(F32)[0:2]
    own_k.wait()
    own_v.wait()
    pl.semaphore_wait(barrier, len(greeted))

    ready, done = [], {}
    for n, key in enumerate(order):
        event(key)
        if n == 1:
            push(halo_out.at[0], halo_in.at[0], h_recv.at[0], right)
            push(halo_out.at[1], halo_in.at[1], h_recv.at[1], left)
            push(rc_ref, rcin, m_recv, mirror)
            for copy in own_q:
                copy.wait()
            prepare()
        if n == 9:
            convolve()
        done[key[2]] = done.get(key[2], 0) + 1
        if done[key[2]] == 2 * NA:
            ready += [(key[2], h) for h in range(0, HEADS, 2)]
        if n < len(order) - 1 and ready:
            dy, h = ready.pop(0)
            if h == 0:
                gather_keys(dy)
            attend(h, h + 2)
    while ready:
        dy, h = ready[0]
        if h == 0:
            gather_keys(dy)
        attend(h, HEADS)
        ready = [r for r in ready if r[0] != dy]

    landed(rcin, m_recv)
    row = lax.broadcasted_iota(jnp.int32, (ROWS, ROWS), 0)
    col = lax.broadcasted_iota(jnp.int32, (ROWS, ROWS), 1)
    turn = jnp.where(row + col == ROWS - 1, 1.0, 0.0).astype(BF16)

    def finish(j, _):
        cols = pl.ds(pl.multiple_of(j * 2 * DV, 128), 2 * DV)
        one, two = acc[2 * j], acc[2 * j + 1]
        attended = jnp.concatenate(
            [one[:, :DV] / one[:, DV : DV + 1], two[:, :DV] / two[:, DV : DV + 1]], axis=1
        )
        grd[8:136, cols] = base[:, cols] + attended - jnp.dot(turn, rcin[:, cols], preferred_element_type=F32)
        return 0

    lax.fori_loop(0, HEADS // 2, finish, 0)
    edge_out[0] = grd[135:136, :]
    edge_out[1] = grd[8:9, :]
    push(edge_out.at[0], edge_in.at[0], e_recv.at[0], right)
    push(edge_out.at[1], edge_in.at[1], e_recv.at[1], left)

    part[:, 30:32, :] = jnp.zeros((2, 2, 128), F32)
    for half in range(2):
        for j in range(6):
            cols = slice((half * 6 + j) * 128, (half * 6 + j + 1) * 128)
            g = grd[8:136, cols]
            taps = (ev[7:135, cols], od[7:135, cols], ev[8:136, cols], od[8:136, cols], ev[9:137, cols])
            part[half, j * KW : (j + 1) * KW, :] = jnp.concatenate(
                [jnp.sum(g * tap, axis=0, keepdims=True) for tap in taps], axis=0
            )
    push(part.at[1 - core], core_in, c_recv.at[0], other_core)

    def spread(low, high):
        def chunk(i, _):
            cols = pl.ds(pl.multiple_of(i * 128, 128), 128)
            w = w_ref[:, cols]
            before, here, after = grd[7:135, cols], grd[8:136, cols], grd[9:137, cols]
            wide[i, pl.ds(0, ROWS, stride=2), :] = w[0:1] * after + w[2:3] * here + w[4:5] * before
            wide[i, pl.ds(1, ROWS, stride=2), :] = w[1:2] * after + w[3:4] * here
            df_ref[:, cols] = wide[i].astype(BF16)
            return 0

        lax.fori_loop(low, high, chunk, 0)

    landed(core_in, c_recv.at[0])
    x_in[x] = part[core] + core_in[...]
    for i, peer in enumerate(x_peers):
        push(x_in.at[x], x_in.at[x], x_recv.at[x], peer)
    landed(edge_in.at[0], e_recv.at[0])
    landed(edge_in.at[1], e_recv.at[1])
    grd[7:8, :] = edge_in[0] * jnp.where(ctx > 0, 1.0, 0.0)
    grd[136:137, :] = edge_in[1] * jnp.where(ctx < count - 1, 1.0, 0.0)
    spread(0, 3)
    for i in range(1, NX):
        slot = lax.rem(x + i, NX)
        landed(x_in.at[slot], x_recv.at[slot])
    z_in[z] = jnp.sum(x_in[...], axis=0)
    for peer in z_peers:
        push(z_in.at[z], z_in.at[z], z_recv.at[z], peer)
    spread(3, 8)
    for i in range(1, NZ):
        slot = lax.rem(z + i, NZ)
        landed(z_in.at[slot], z_recv.at[slot])
    y_in[y] = jnp.sum(z_in[...], axis=0)
    for peer in y_peers:
        push(y_in.at[y], y_in.at[y], y_recv.at[y], peer)
    spread(8, 12)
    for i in range(1, NY):
        slot = lax.rem(y + i, NY)
        landed(y_in.at[slot], y_recv.at[slot])
    final[core] = jnp.sum(y_in[...], axis=0) * (1.0 / math.sqrt(NX * 4 * count * ROWS))
    push(final.at[core], final.at[core], c_recv.at[1], other_core)
    landed(final.at[1 - core], c_recv.at[1])
    for half in range(2):
        for j in range(6):
            cols = slice((half * 6 + j) * 128, (half * 6 + j + 1) * 128)
            dw_ref[:, cols] = final[half, j * KW : (j + 1) * KW, :]
    for copy in started:
        copy.wait_send()


def run(queries, keys, values, features_fine, rc_state, conv_weight):
    vmem, hbm = pl.BlockSpec(memory_space=pltpu.VMEM), pl.BlockSpec(memory_space=pltpu.HBM)
    dma = pltpu.SemaphoreType.DMA
    n_sends = sum(len(s) for s in block_sends().values()) + 3 + 2 + 1 + 3 + 7 + 7 + 1
    return pl.pallas_call(
        kernel,
        name="attend_and_convolve",
        out_shape=(jax.ShapeDtypeStruct((2 * ROWS, D), BF16), jax.ShapeDtypeStruct((KW, D), F32)),
        in_specs=[hbm] * 5 + [vmem],
        out_specs=(vmem, vmem),
        scratch_shapes=[
            pltpu.VMEM((NY, NA, ROWS, DK), BF16),
            pltpu.VMEM((NY, NA, DV, 128), BF16),
            pltpu.VMEM((ROWS, D), BF16),
            pltpu.VMEM((HEADS, ROWS, DK), BF16),
            pltpu.VMEM((DK, NA * ROWS), BF16),
            pltpu.VMEM((NA * ROWS, 256), BF16),
            pltpu.VMEM((HEADS, ROWS, 128), F32),
            pltpu.VMEM((HEADS, ROWS, 256), F32),
            pltpu.VMEM((2 * ROWS, D), BF16),
            pltpu.VMEM((D // 128, 2 * ROWS, 128), F32),
            pltpu.VMEM((ROWS, D), F32),
            pltpu.VMEM((ROWS + 16, D), F32),
            pltpu.VMEM((ROWS + 16, D), F32),
            pltpu.VMEM((ROWS + 16, D), F32),
            pltpu.VMEM((2, 2, D), F32),
            pltpu.VMEM((2, 2, D), F32),
            pltpu.VMEM((2, 1, D), F32),
            pltpu.VMEM((2, 1, D), F32),
            pltpu.VMEM((2, 32, 128), F32),
            pltpu.VMEM((32, 128), F32),
            pltpu.VMEM((NX, 32, 128), F32),
            pltpu.VMEM((NZ, 32, 128), F32),
            pltpu.VMEM((NY, 32, 128), F32),
            pltpu.VMEM((2, 32, 128), F32),
            dma((11,)),
            dma((n_sends,)),
            dma((NY, NA)),
            dma((NY, NA)),
            dma,
            dma((2,)),
            dma((2,)),
            dma((2,)),
            dma((NX,)),
            dma((NZ,)),
            dma((NY,)),
        ],
        compiler_params=pltpu.CompilerParams(
            collective_id=0, has_side_effects=True, vmem_limit_bytes=40 * 2**20
        ),
    )(queries, keys, values, features_fine, rc_state, conv_weight)


def body(queries, keys, values, features_fine, rc_state, conv_weight):
    d_fine, d_weight = run(
        queries[0], keys[0], jnp.swapaxes(values[0], 0, 1), features_fine[0], rc_state[0], conv_weight
    )
    return d_fine[None], d_weight


def solution(mesh):
    split = P("dp", "ctx", None)
    return jax.shard_map(
        body, mesh=mesh, in_specs=(split,) * 5 + (P(),), out_specs=(split, P()), check_vma=False
    )
```

```python
import heapq
import math

import jax
import jax.numpy as jnp
from jax import lax
from jax.experimental import pallas as pl
from jax.experimental.pallas import tpu as pltpu
from jax.sharding import PartitionSpec as P

HEADS = 8
DK = 128
DV = 192
ROWS = 128
D = HEADS * DV
KW = 5
KVROWS = DK + DV
KPART = 128
PIECES = 4
NA, NY = 4, 8
NX, NZ = 4, 8
MESH = pl.DeviceIdType.MESH
F32 = jnp.float32
BF16 = jnp.bfloat16


def block_sends():
    sends = {}
    for za in range(NA):
        cw = 4 - za % 2
        for dy in range(NY):
            behind = (NY - dy) % NY
            v, k = [], []
            if dy == 0:
                if za == 0:
                    v += [("near", ("V", 1, 0)), ("far", ("V", 2, 0))]
                if za == 2:
                    v.append(("near", ("V", 3, 0)))
                v += [("y+", ("V", za, 7)), ("y-", ("V", za, 1))]
            elif behind <= cw:
                if behind < cw:
                    v.append(("y+", ("V", za, dy - 1)))
            elif dy < 7 - cw:
                v.append(("y-", ("V", za, dy + 1)))
            sends[("V", za, dy)] = v
            if za == 0:
                if dy == 0:
                    k += [("y+", ("K", 0, 7)), ("y-", ("K", 0, 1))]
                elif behind < 4:
                    k.append(("y+", ("K", 0, dy - 1)))
                elif dy < 3:
                    k.append(("y-", ("K", 0, dy + 1)))
                k += [("near", ("K", 1, dy)), ("far", ("K", 2, dy))]
            elif za == 2:
                k.append(("near", ("K", 3, dy)))
            sends[("K", za, dy)] = k
    return sends


def arrival_order(sends):
    free = {"y+": 0.0, "y-": 0.0, "near": 0.0, "far": 0.0}
    slow = {"y+": 1.5, "y-": 1.5, "near": 2.0, "far": 4.0}
    cost = {"V": (KVROWS - KPART) * 0.0055, "K": KPART * 0.0055}
    queue = [(0.0, 0, ("V", 0, 0)), (0.0, 1, ("K", 0, 0))]
    order, n = [], 2
    while queue:
        now, _, key = heapq.heappop(queue)
        order.append(key)
        for link, child in sends[key]:
            end = max(now, free[link]) + cost[key[0]] * slow[link]
            free[link] = end
            heapq.heappush(queue, (end + (1.8 if link[0] == "y" else 2.4), n, child))
            n += 1
    return order


def kernel(
    q_ref, k_ref, v_ref, ff_ref, rc_ref, w_ref, df_ref, dw_ref,
    kv, relay, rcin, qs, kx, vx, top, acc, fine, wide, base, ev, od, grd, halo_out, halo_in, edge_out, edge_in,
    part, core_in, x_in, z_in, y_in, final,
    local, send_sem, k_sem, v_sem, m_sem, h_recv, e_recv, c_recv, x_recv, z_recv, y_recv,
):
    dp, ctx = lax.axis_index("dp"), lax.axis_index("ctx")
    a, y = ctx // NY, lax.rem(ctx, NY)
    core, zlo, x = lax.rem(dp, 2), lax.rem(dp // 2, 2), dp // 4
    z = a * 2 + zlo
    count = NA * NY

    def at(a_new, y_new):
        return (dp, lax.rem(a_new, NA) * NY + lax.rem(y_new, NY))

    right, left = (dp, lax.rem(ctx + 1, count)), (dp, lax.rem(ctx + count - 1, count))
    near, far = a + 1 - 2 * lax.rem(a, 2), NA - 1 - a
    rows_of_a = (a, near, far, NA - 1 - near)
    y_mirror = (dp, a * NY + NY - 1 - y)
    peers = {"y+": at(a, y + 1), "y-": at(a, y + NY - 1), "near": at(near, y), "far": at(far, y)}
    other_core = (dp + 1 - 2 * core, ctx)
    x_peers = [(lax.rem(x + i, NX) * 4 + zlo * 2 + core, ctx) for i in range(1, NX)]
    z_peers = []
    for i in range(1, NZ):
        z_new = lax.rem(z + i, NZ)
        z_peers.append((x * 4 + lax.rem(z_new, 2) * 2 + core, z_new // 2 * NY + y))
    y_peers = [at(a, y + i) for i in range(1, NY)]
    barrier = pltpu.get_barrier_semaphore()
    greeted = [right, left, y_mirror, other_core] + x_peers + z_peers + y_peers
    for peer in greeted:
        pl.semaphore_signal(barrier, inc=1, device_id=peer, device_id_type=MESH)

    own_k = pltpu.make_async_copy(k_ref, kv.at[y, a, pl.ds(0, DK)], local.at[0])
    own_v = pltpu.make_async_copy(v_ref, kv.at[y, a, pl.ds(DK, DV)], local.at[1])
    own_f = pltpu.make_async_copy(ff_ref, fine, local.at[2])
    own_q = [
        pltpu.make_async_copy(q_ref.at[:, pl.ds(h * DK, DK)], qs.at[h], local.at[3 + h]) for h in range(HEADS)
    ]
    for copy in [own_f, own_k, own_v] + own_q:
        copy.start()

    started = []

    def push(src, dst, recv_sem, peer):
        copy = pltpu.make_async_remote_copy(
            src, dst, send_sem.at[len(started)], recv_sem, device_id=peer, device_id_type=MESH
        )
        copy.start()
        started.append(copy)

    def landed(ref, sem):
        pltpu.make_async_remote_copy(ref, ref, sem, sem, device_id=other_core, device_id_type=MESH).wait_recv()

    sends = block_sends()
    order = arrival_order(sends)

    def event(key):
        o_a, o_y = rows_of_a[key[1]], lax.rem(y + key[2], NY)
        if key[0] == "K":
            ref, sem = kv.at[o_y, o_a, pl.ds(0, KPART)], k_sem.at[o_y, o_a]
        else:
            ref, sem = kv.at[o_y, o_a, pl.ds(KPART, KVROWS - KPART)], v_sem.at[o_y, o_a]
        if key[1:] != (0, 0):
            landed(ref, sem)
        for link, _ in sends[key]:
            push(ref, ref, sem, peers[link])

    step = ROWS // 2 // PIECES

    def lanes(i):
        one, two = pl.ds(i * step, step), pl.ds(ROWS // 2 + i * step, step)
        return ((one, 0, y_mirror, peers["far"]), (two, 1, peers["far"], y_mirror))

    def reflect(i):
        for rows, way, peer, _ in lanes(i):
            push(rc_ref.at[rows], relay.at[rows], m_sem.at[way, i], peer)

    def reflect_on(i):
        for rows, way, _, peer in lanes(i):
            landed(relay.at[rows], m_sem.at[way, i])
            push(relay.at[rows], rcin.at[rows], m_sem.at[2 + way, i], peer)

    def reflected(i):
        for rows, way, _, _ in lanes(i):
            landed(rcin.at[rows], m_sem.at[2 + way, i])

    def prepare():
        def heads(h, _):
            top[h] = jnp.full((ROWS, 128), -1e30, F32)
            acc[h] = jnp.zeros((ROWS, 256), F32)
            return 0

        lax.fori_loop(0, HEADS, heads, 0)
        vx[:, DV:256] = jnp.ones((NA * ROWS, 64), BF16)

    def gather_keys(dy):
        o_y = lax.rem(y + dy, NY)
        for i in range(NA):
            rows = slice(i * ROWS, (i + 1) * ROWS)
            kx[:, rows] = kv[o_y, i, 0:DK, :].T
            vx[rows, 0:128] = kv[o_y, i, DK : DK + 128, :].T
            vx[rows, 128:192] = kv[o_y, i, DK + 128 : DK + DV, :].T

    factor = DK ** (-0.5) * math.log2(math.e)

    def attend():
        s = jnp.dot(qs[...].reshape(HEADS * ROWS, DK), kx[...], preferred_element_type=F32)
        old = top[...].reshape(HEADS * ROWS, 128)
        new = jnp.maximum(old, jnp.max(s, axis=1, keepdims=True))
        p = jnp.exp2((s - new[:, :1]) * factor).astype(BF16)
        fade = jnp.exp2((old - new) * factor)
        fade = jnp.concatenate([fade, fade], axis=1)
        total = acc[...].reshape(HEADS * ROWS, 256) * fade + jnp.dot(p, vx[...], preferred_element_type=F32)
        acc[...] = total.reshape(HEADS, ROWS, 256)
        top[...] = new.reshape(HEADS, ROWS, 128)

    def widen():
        def chunk(i, _):
            cols = pl.ds(pl.multiple_of(i * 128, 128), 128)
            wide[i] = fine[:, cols].astype(F32)
            ev[8:136, cols] = wide[i, pl.ds(0, ROWS, stride=2), :]
            od[8:136, cols] = wide[i, pl.ds(1, ROWS, stride=2), :]
            return 0

        lax.fori_loop(0, D // 128, chunk, 0)

    def take_halo():
        landed(halo_in.at[0], h_recv.at[0])
        landed(halo_in.at[1], h_recv.at[1])
        inner_left = jnp.where(ctx > 0, 1.0, 0.0)
        inner_right = jnp.where(ctx < count - 1, 1.0, 0.0)
        ev[7:8, :] = halo_in[0, 0:1, :] * inner_left
        od[7:8, :] = halo_in[0, 1:2, :] * inner_left
        ev[136:137, :] = halo_in[1, 0:1, :] * inner_right

    def convolve(low, high):
        def chunk(i, _):
            cols = pl.ds(pl.multiple_of(i * 128, 128), 128)
            w = w_ref[:, cols]
            base[:, cols] = (
                w[0:1] * ev[7:135, cols]
                + w[1:2] * od[7:135, cols]
                + w[2:3] * ev[8:136, cols]
                + w[3:4] * od[8:136, cols]
                + w[4:5] * ev[9:137, cols]
            )
            return 0

        lax.fori_loop(low, high, chunk, 0)

    own_f.wait()
    halo_out[0] = fine[2 * ROWS - 16 : 2 * ROWS, :].astype(F32)[14:16]
    halo_out[1] = fine[0:16, :].astype(F32)[0:2]
    own_k.wait()
    own_v.wait()
    pl.semaphore_wait(barrier, len(greeted))

    ready, done = [], {}
    out, back = 0, 0
    for n, key in enumerate(order):
        event(key)
        if out < PIECES and n >= 1 + out * 8:
            reflect(out)
            out += 1
        if n == 1:
            push(halo_out.at[0], halo_in.at[0], h_recv.at[0], right)
            push(halo_out.at[1], halo_in.at[1], h_recv.at[1], left)
            for copy in own_q:
                copy.wait()
            prepare()
            widen()
        if back < out and n >= 20 + back * 12:
            reflect_on(back)
            back += 1
        if n == 7:
            take_halo()
        if n in (8, 10, 12, 14):
            convolve((n - 8) // 2 * 3, (n - 8) // 2 * 3 + 3)
        done[key[2]] = done.get(key[2], 0) + 1
        if done[key[2]] == 2 * NA:
            ready.append(key[2])
        if ready:
            gather_keys(ready.pop(0))
            attend()
    for i in range(back, PIECES):
        reflect_on(i)
    for i in range(PIECES):
        reflected(i)
    row = lax.broadcasted_iota(jnp.int32, (ROWS, ROWS), 0)
    col = lax.broadcasted_iota(jnp.int32, (ROWS, ROWS), 1)
    turn = jnp.where(row + col == ROWS - 1, 1.0, 0.0).astype(BF16)

    def finish(j, _):
        cols = pl.ds(pl.multiple_of(j * 2 * DV, 128), 2 * DV)
        one, two = acc[2 * j], acc[2 * j + 1]
        attended = jnp.concatenate(
            [one[:, :DV] / one[:, DV : DV + 1], two[:, :DV] / two[:, DV : DV + 1]], axis=1
        )
        grd[8:136, cols] = base[:, cols] + attended - jnp.dot(turn, rcin[:, cols], preferred_element_type=F32)
        return 0

    lax.fori_loop(0, HEADS // 2, finish, 0)
    edge_out[0] = grd[135:136, :]
    edge_out[1] = grd[8:9, :]
    push(edge_out.at[0], edge_in.at[0], e_recv.at[0], right)
    push(edge_out.at[1], edge_in.at[1], e_recv.at[1], left)

    part[:, 30:32, :] = jnp.zeros((2, 2, 128), F32)
    for half in range(2):
        for j in range(6):
            cols = slice((half * 6 + j) * 128, (half * 6 + j + 1) * 128)
            g = grd[8:136, cols]
            taps = (ev[7:135, cols], od[7:135, cols], ev[8:136, cols], od[8:136, cols], ev[9:137, cols])
            part[half, j * KW : (j + 1) * KW, :] = jnp.concatenate(
                [jnp.sum(g * tap, axis=0, keepdims=True) for tap in taps], axis=0
            )
    push(part.at[1 - core], core_in, c_recv.at[0], other_core)

    def spread(low, high):
        def chunk(i, _):
            cols = pl.ds(pl.multiple_of(i * 128, 128), 128)
            w = w_ref[:, cols]
            before, here, after = grd[7:135, cols], grd[8:136, cols], grd[9:137, cols]
            wide[i, pl.ds(0, ROWS, stride=2), :] = w[0:1] * after + w[2:3] * here + w[4:5] * before
            wide[i, pl.ds(1, ROWS, stride=2), :] = w[1:2] * after + w[3:4] * here
            df_ref[:, cols] = wide[i].astype(BF16)
            return 0

        lax.fori_loop(low, high, chunk, 0)

    landed(core_in, c_recv.at[0])
    x_in[x] = part[core] + core_in[...]
    for i, peer in enumerate(x_peers):
        push(x_in.at[x], x_in.at[x], x_recv.at[x], peer)
    landed(edge_in.at[0], e_recv.at[0])
    landed(edge_in.at[1], e_recv.at[1])
    grd[7:8, :] = edge_in[0] * jnp.where(ctx > 0, 1.0, 0.0)
    grd[136:137, :] = edge_in[1] * jnp.where(ctx < count - 1, 1.0, 0.0)
    spread(0, 3)
    for i in range(1, NX):
        slot = lax.rem(x + i, NX)
        landed(x_in.at[slot], x_recv.at[slot])
    z_in[z] = jnp.sum(x_in[...], axis=0)
    for peer in z_peers:
        push(z_in.at[z], z_in.at[z], z_recv.at[z], peer)
    spread(3, 8)
    for i in range(1, NZ):
        slot = lax.rem(z + i, NZ)
        landed(z_in.at[slot], z_recv.at[slot])
    y_in[y] = jnp.sum(z_in[...], axis=0)
    for peer in y_peers:
        push(y_in.at[y], y_in.at[y], y_recv.at[y], peer)
    spread(8, 12)
    for i in range(1, NY):
        slot = lax.rem(y + i, NY)
        landed(y_in.at[slot], y_recv.at[slot])
    final[core] = jnp.sum(y_in[...], axis=0) * (1.0 / math.sqrt(NX * 4 * count * ROWS))
    push(final.at[core], final.at[core], c_recv.at[1], other_core)
    landed(final.at[1 - core], c_recv.at[1])
    for half in range(2):
        for j in range(6):
            cols = slice((half * 6 + j) * 128, (half * 6 + j + 1) * 128)
            dw_ref[:, cols] = final[half, j * KW : (j + 1) * KW, :]
    for copy in started:
        copy.wait_send()


def run(queries, keys, values, features_fine, rc_state, conv_weight):
    vmem, hbm = pl.BlockSpec(memory_space=pltpu.VMEM), pl.BlockSpec(memory_space=pltpu.HBM)
    dma = pltpu.SemaphoreType.DMA
    n_sends = sum(len(s) for s in block_sends().values()) + 4 * PIECES + 2 + 2 + 1 + 3 + 7 + 7 + 1
    return pl.pallas_call(
        kernel,
        name="attend_and_convolve",
        out_shape=(jax.ShapeDtypeStruct((2 * ROWS, D), BF16), jax.ShapeDtypeStruct((KW, D), F32)),
        in_specs=[hbm] * 5 + [vmem],
        out_specs=(vmem, vmem),
        scratch_shapes=[
            pltpu.VMEM((NY, NA, KVROWS, 128), BF16),
            pltpu.VMEM((ROWS, D), BF16),
            pltpu.VMEM((ROWS, D), BF16),
            pltpu.VMEM((HEADS, ROWS, DK), BF16),
            pltpu.VMEM((DK, NA * ROWS), BF16),
            pltpu.VMEM((NA * ROWS, 256), BF16),
            pltpu.VMEM((HEADS, ROWS, 128), F32),
            pltpu.VMEM((HEADS, ROWS, 256), F32),
            pltpu.VMEM((2 * ROWS, D), BF16),
            pltpu.VMEM((D // 128, 2 * ROWS, 128), F32),
            pltpu.VMEM((ROWS, D), F32),
            pltpu.VMEM((ROWS + 16, D), F32),
            pltpu.VMEM((ROWS + 16, D), F32),
            pltpu.VMEM((ROWS + 16, D), F32),
            pltpu.VMEM((2, 2, D), F32),
            pltpu.VMEM((2, 2, D), F32),
            pltpu.VMEM((2, 1, D), F32),
            pltpu.VMEM((2, 1, D), F32),
            pltpu.VMEM((2, 32, 128), F32),
            pltpu.VMEM((32, 128), F32),
            pltpu.VMEM((NX, 32, 128), F32),
            pltpu.VMEM((NZ, 32, 128), F32),
            pltpu.VMEM((NY, 32, 128), F32),
            pltpu.VMEM((2, 32, 128), F32),
            dma((11,)),
            dma((n_sends,)),
            dma((NY, NA)),
            dma((NY, NA)),
            dma((4, PIECES)),
            dma((2,)),
            dma((2,)),
            dma((2,)),
            dma((NX,)),
            dma((NZ,)),
            dma((NY,)),
        ],
        compiler_params=pltpu.CompilerParams(
            collective_id=0, has_side_effects=True, vmem_limit_bytes=62 * 2**20
        ),
    )(queries, keys, values, features_fine, rc_state, conv_weight)


def body(queries, keys, values, features_fine, rc_state, conv_weight):
    d_fine, d_weight = run(
        queries[0], keys[0], jnp.swapaxes(values[0], 0, 1), features_fine[0], rc_state[0], conv_weight
    )
    return d_fine[None], d_weight


def solution(mesh):
    split = P("dp", "ctx", None)
    return jax.shard_map(
        body, mesh=mesh, in_specs=(split,) * 5 + (P(),), out_specs=(split, P()), check_vma=False
    )
```

```python
import heapq
import math

import jax
import jax.numpy as jnp
from jax import lax
from jax.experimental import pallas as pl
from jax.experimental.pallas import tpu as pltpu
from jax.sharding import PartitionSpec as P

HEADS = 8
DK = 128
DV = 192
ROWS = 128
D = HEADS * DV
KW = 5
KVROWS = DK + DV
KPART = 112
PIECES = 4
NA, NY = 4, 8
NX, NZ = 4, 8
MESH = pl.DeviceIdType.MESH
F32 = jnp.float32
BF16 = jnp.bfloat16


def block_sends():
    sends = {}
    for za in range(NA):
        cw = 4 - za % 2
        for dy in range(NY):
            behind = (NY - dy) % NY
            v, k = [], []
            if dy == 0:
                if za == 0:
                    v += [("near", ("V", 1, 0)), ("far", ("V", 2, 0))]
                if za == 2:
                    v.append(("near", ("V", 3, 0)))
                v += [("y+", ("V", za, 7)), ("y-", ("V", za, 1))]
            elif behind <= cw:
                if behind < cw:
                    v.append(("y+", ("V", za, dy - 1)))
            elif dy < 7 - cw:
                v.append(("y-", ("V", za, dy + 1)))
            sends[("V", za, dy)] = v
            if za == 0:
                if dy == 0:
                    k += [("y+", ("K", 0, 7)), ("y-", ("K", 0, 1))]
                elif behind < 4:
                    k.append(("y+", ("K", 0, dy - 1)))
                elif dy < 3:
                    k.append(("y-", ("K", 0, dy + 1)))
                k += [("near", ("K", 1, dy)), ("far", ("K", 2, dy))]
            elif za == 2:
                k.append(("near", ("K", 3, dy)))
            sends[("K", za, dy)] = k
    return sends


def arrival_order(sends):
    free = {"y+": 0.0, "y-": 0.0, "near": 0.0, "far": 0.0}
    slow = {"y+": 1.5, "y-": 1.5, "near": 2.0, "far": 4.0}
    cost = {"V": (KVROWS - KPART) * 0.0055, "K": KPART * 0.0055}
    queue = [(0.0, 0, ("V", 0, 0)), (0.0, 1, ("K", 0, 0))]
    order, n = [], 2
    while queue:
        now, _, key = heapq.heappop(queue)
        order.append(key)
        for link, child in sends[key]:
            end = max(now, free[link]) + cost[key[0]] * slow[link]
            free[link] = end
            heapq.heappush(queue, (end + (1.8 if link[0] == "y" else 2.4), n, child))
            n += 1
    return order


def kernel(
    q_ref, k_ref, v_ref, ff_ref, rc_ref, cw_ref, df_ref, dw_ref,
    w_ref, kv, relay, rcin, qs, kx, vx, top, acc, fine, wide, base, ev, od, grd, halo_out, halo_in, edge_out, edge_in,
    part, e_in, z_in, y_in, final,
    local, send_sem, k_sem, v_sem, m_sem, h_recv, e_recv, s_send, s_recv, z_recv, y_recv, f_recv,
):
    dp, ctx = lax.axis_index("dp"), lax.axis_index("ctx")
    a, y = ctx // NY, lax.rem(ctx, NY)
    core, zlo, x = lax.rem(dp, 2), lax.rem(dp // 2, 2), dp // 4
    z = a * 2 + zlo
    count = NA * NY

    def at(a_new, y_new):
        return (dp, lax.rem(a_new, NA) * NY + lax.rem(y_new, NY))

    right, left = (dp, lax.rem(ctx + 1, count)), (dp, lax.rem(ctx + count - 1, count))
    near, far = a + 1 - 2 * lax.rem(a, 2), NA - 1 - a
    rows_of_a = (a, near, far, NA - 1 - near)
    y_mirror = (dp, a * NY + NY - 1 - y)
    peers = {"y+": at(a, y + 1), "y-": at(a, y + NY - 1), "near": at(near, y), "far": at(far, y)}
    other_core = (dp + 1 - 2 * core, ctx)
    e = x * 2 + core
    e_peers = []
    for i in range(1, 8):
        e_new = lax.rem(e + i, 8)
        e_peers.append((e_new // 2 * 4 + zlo * 2 + lax.rem(e_new, 2), ctx))
    z_peers = []
    for i in range(1, NZ):
        z_new = lax.rem(z + i, NZ)
        z_peers.append((x * 4 + lax.rem(z_new, 2) * 2 + core, z_new // 2 * NY + y))
    y_peers = [at(a, y + i) for i in range(1, NY)]
    barrier = pltpu.get_barrier_semaphore()
    greeted = [right, left, y_mirror] + e_peers + z_peers + y_peers
    for peer in greeted:
        pl.semaphore_signal(barrier, inc=1, device_id=peer, device_id_type=MESH)

    own_k = pltpu.make_async_copy(k_ref, kv.at[y, a, pl.ds(0, DK)], local.at[0])
    own_v = pltpu.make_async_copy(v_ref, kv.at[y, a, pl.ds(DK, DV)], local.at[1])
    own_f = pltpu.make_async_copy(ff_ref, fine, local.at[2])
    own_q = [
        pltpu.make_async_copy(q_ref.at[:, pl.ds(h * DK, DK)], qs.at[h], local.at[3 + h]) for h in range(HEADS)
    ]
    own_w = pltpu.make_async_copy(cw_ref, w_ref, local.at[3 + HEADS])
    for copy in [own_f, own_k, own_v] + own_q + [own_w]:
        copy.start()

    started = []

    def push(src, dst, recv_sem, peer):
        copy = pltpu.make_async_remote_copy(
            src, dst, send_sem.at[len(started)], recv_sem, device_id=peer, device_id_type=MESH
        )
        copy.start()
        started.append(copy)

    def landed(ref, sem):
        pltpu.make_async_remote_copy(ref, ref, sem, sem, device_id=other_core, device_id_type=MESH).wait_recv()

    sends = block_sends()
    order = arrival_order(sends)

    def event(key):
        o_a, o_y = rows_of_a[key[1]], lax.rem(y + key[2], NY)
        if key[0] == "K":
            ref, sem = kv.at[o_y, o_a, pl.ds(0, KPART)], k_sem.at[o_y, o_a]
        else:
            ref, sem = kv.at[o_y, o_a, pl.ds(KPART, KVROWS - KPART)], v_sem.at[o_y, o_a]
        if key[1:] != (0, 0):
            landed(ref, sem)
        for link, _ in sends[key]:
            push(ref, ref, sem, peers[link])

    step = ROWS // 2 // PIECES

    def lanes(i):
        one, two = pl.ds(i * step, step), pl.ds(ROWS // 2 + i * step, step)
        return ((one, 0, y_mirror, peers["far"]), (two, 1, peers["far"], y_mirror))

    def reflect(i):
        for rows, way, peer, _ in lanes(i):
            push(rc_ref.at[rows], relay.at[rows], m_sem.at[way, i], peer)

    def reflect_on(i):
        for rows, way, _, peer in lanes(i):
            landed(relay.at[rows], m_sem.at[way, i])
            push(relay.at[rows], rcin.at[rows], m_sem.at[2 + way, i], peer)

    def reflected(i):
        for rows, way, _, _ in lanes(i):
            landed(rcin.at[rows], m_sem.at[2 + way, i])

    def prepare():
        def heads(h, _):
            top[h] = jnp.full((ROWS, 128), -1e30, F32)
            acc[h] = jnp.zeros((ROWS, 256), F32)
            return 0

        lax.fori_loop(0, HEADS, heads, 0)
        vx[:, DV:256] = jnp.ones((NA * ROWS, 64), BF16)

    def gather_keys(dy):
        o_y = lax.rem(y + dy, NY)
        for i in range(NA):
            rows = slice(i * ROWS, (i + 1) * ROWS)
            kx[:, rows] = kv[o_y, i, 0:DK, :].T
            vx[rows, 0:128] = kv[o_y, i, DK : DK + 128, :].T
            vx[rows, 128:192] = kv[o_y, i, DK + 128 : DK + DV, :].T

    factor = DK ** (-0.5) * math.log2(math.e)

    def attend():
        s = jnp.dot(qs[...].reshape(HEADS * ROWS, DK), kx[...], preferred_element_type=F32)
        old = top[...].reshape(HEADS * ROWS, 128)
        new = jnp.maximum(old, jnp.max(s, axis=1, keepdims=True))
        p = jnp.exp2((s - new[:, :1]) * factor).astype(BF16)
        fade = jnp.exp2((old - new) * factor)
        fade = jnp.concatenate([fade, fade], axis=1)
        total = acc[...].reshape(HEADS * ROWS, 256) * fade + jnp.dot(p, vx[...], preferred_element_type=F32)
        acc[...] = total.reshape(HEADS, ROWS, 256)
        top[...] = new.reshape(HEADS, ROWS, 128)

    def widen():
        def chunk(i, _):
            cols = pl.ds(pl.multiple_of(i * 128, 128), 128)
            wide[i] = fine[:, cols].astype(F32)
            ev[8:136, cols] = wide[i, pl.ds(0, ROWS, stride=2), :]
            od[8:136, cols] = wide[i, pl.ds(1, ROWS, stride=2), :]
            return 0

        lax.fori_loop(0, D // 128, chunk, 0)

    def take_halo():
        landed(halo_in.at[0], h_recv.at[0])
        landed(halo_in.at[1], h_recv.at[1])
        inner_left = jnp.where(ctx > 0, 1.0, 0.0)
        inner_right = jnp.where(ctx < count - 1, 1.0, 0.0)
        ev[7:8, :] = halo_in[0, 0:1, :] * inner_left
        od[7:8, :] = halo_in[0, 1:2, :] * inner_left
        ev[136:137, :] = halo_in[1, 0:1, :] * inner_right

    def convolve(low, high):
        def chunk(i, _):
            cols = pl.ds(pl.multiple_of(i * 128, 128), 128)
            w = w_ref[:, cols]
            base[:, cols] = (
                w[0:1] * ev[7:135, cols]
                + w[1:2] * od[7:135, cols]
                + w[2:3] * ev[8:136, cols]
                + w[3:4] * od[8:136, cols]
                + w[4:5] * ev[9:137, cols]
            )
            return 0

        lax.fori_loop(low, high, chunk, 0)

    own_f.wait()
    halo_out[0] = fine[2 * ROWS - 16 : 2 * ROWS, :].astype(F32)[14:16]
    halo_out[1] = fine[0:16, :].astype(F32)[0:2]
    own_k.wait()
    own_v.wait()
    pl.semaphore_wait(barrier, len(greeted))

    ready, done = [], {}
    out, back = 0, 0
    for n, key in enumerate(order):
        event(key)
        if out < PIECES and n >= 1 + out * 8:
            reflect(out)
            out += 1
        if n == 1:
            push(halo_out.at[0], halo_in.at[0], h_recv.at[0], right)
            push(halo_out.at[1], halo_in.at[1], h_recv.at[1], left)
            for copy in own_q + [own_w]:
                copy.wait()
            prepare()
            widen()
        if back < out and n >= 20 + back * 12:
            reflect_on(back)
            back += 1
        if n == 7:
            take_halo()
        if n in (8, 10, 12, 14):
            convolve((n - 8) // 2 * 3, (n - 8) // 2 * 3 + 3)
        done[key[2]] = done.get(key[2], 0) + 1
        if done[key[2]] == 2 * NA:
            ready.append(key[2])
        if ready and (n > len(order) - 2 or (done[key[2]] != 2 * NA)):
            gather_keys(ready.pop(0))
            attend()
    while ready:
        gather_keys(ready.pop(0))
        attend()
    for i in range(back, PIECES):
        reflect_on(i)
    for i in range(PIECES):
        reflected(i)
    row = lax.broadcasted_iota(jnp.int32, (ROWS, ROWS), 0)
    col = lax.broadcasted_iota(jnp.int32, (ROWS, ROWS), 1)
    turn = jnp.where(row + col == ROWS - 1, 1.0, 0.0).astype(BF16)

    part[60:64, :] = jnp.zeros((4, 128), F32)
    shared, given = [], 0
    for j in range(HEADS // 2):
        cols = slice(j * 2 * DV, (j + 1) * 2 * DV)
        one, two = acc[2 * j], acc[2 * j + 1]
        attended = jnp.concatenate(
            [one[:, :DV] / one[:, DV : DV + 1], two[:, :DV] / two[:, DV : DV + 1]], axis=1
        )
        grd[8:136, cols] = base[:, cols] + attended - jnp.dot(turn, rcin[:, cols], preferred_element_type=F32)
        for i in range(3 * j, 3 * j + 3):
            cols = slice(i * 128, (i + 1) * 128)
            g = grd[8:136, cols]
            taps = (ev[7:135, cols], od[7:135, cols], ev[8:136, cols], od[8:136, cols], ev[9:137, cols])
            part[i * KW : (i + 1) * KW, :] = jnp.concatenate(
                [jnp.sum(g * tap, axis=0, keepdims=True) for tap in taps], axis=0
            )
        while given < 8 and (8 * given + 8 <= 15 * (j + 1) or j == 3):
            copy = pltpu.make_async_remote_copy(
                part.at[pl.ds(8 * given, 8)], e_in.at[e], s_send.at[given], s_recv.at[e],
                device_id=(given // 2 * 4 + zlo * 2 + given % 2, ctx), device_id_type=MESH,
            )
            pl.when(e != given)(copy.start)
            shared.append(copy)
            given += 1
    edge_out[0] = grd[135:136, :]
    edge_out[1] = grd[8:9, :]
    push(edge_out.at[0], edge_in.at[0], e_recv.at[0], right)
    push(edge_out.at[1], edge_in.at[1], e_recv.at[1], left)

    def spread(low, high):
        def chunk(i, _):
            cols = pl.ds(pl.multiple_of(i * 128, 128), 128)
            w = w_ref[:, cols]
            before, here, after = grd[7:135, cols], grd[8:136, cols], grd[9:137, cols]
            wide[i, pl.ds(0, ROWS, stride=2), :] = w[0:1] * after + w[2:3] * here + w[4:5] * before
            wide[i, pl.ds(1, ROWS, stride=2), :] = w[1:2] * after + w[3:4] * here
            df_ref[:, cols] = wide[i].astype(BF16)
            return 0

        lax.fori_loop(low, high, chunk, 0)

    e_in[e] = part[pl.ds(pl.multiple_of(8 * e, 8), 8), :]
    for i in range(1, 8):
        slot = lax.rem(e + i, 8)
        landed(e_in.at[slot], s_recv.at[slot])
    z_in[z] = jnp.sum(e_in[...], axis=0)
    for peer in z_peers:
        push(z_in.at[z], z_in.at[z], z_recv.at[z], peer)
    landed(edge_in.at[0], e_recv.at[0])
    landed(edge_in.at[1], e_recv.at[1])
    grd[7:8, :] = edge_in[0] * jnp.where(ctx > 0, 1.0, 0.0)
    grd[136:137, :] = edge_in[1] * jnp.where(ctx < count - 1, 1.0, 0.0)
    spread(0, 6)
    for i in range(1, NZ):
        slot = lax.rem(z + i, NZ)
        landed(z_in.at[slot], z_recv.at[slot])
    y_in[y] = jnp.sum(z_in[...], axis=0)
    for peer in y_peers:
        push(y_in.at[y], y_in.at[y], y_recv.at[y], peer)
    spread(6, 12)
    for i in range(1, NY):
        slot = lax.rem(y + i, NY)
        landed(y_in.at[slot], y_recv.at[slot])
    final[pl.ds(pl.multiple_of(8 * e, 8), 8), :] = jnp.sum(y_in[...], axis=0) * (1.0 / math.sqrt(NX * 4 * count * ROWS))
    mine = final.at[pl.ds(pl.multiple_of(8 * e, 8), 8)]
    for peer in e_peers:
        push(mine, mine, f_recv.at[e], peer)
    for i in range(1, 8):
        slot = lax.rem(e + i, 8)
        landed(final.at[pl.ds(pl.multiple_of(8 * slot, 8), 8)], f_recv.at[slot])
    for i in range(D // 128):
        dw_ref[:, i * 128 : (i + 1) * 128] = final[i * KW : (i + 1) * KW, :]
    for i, copy in enumerate(shared):
        pl.when(e != i)(copy.wait_send)
    for copy in started:
        copy.wait_send()


def run(queries, keys, values, features_fine, rc_state, conv_weight):
    vmem, hbm = pl.BlockSpec(memory_space=pltpu.VMEM), pl.BlockSpec(memory_space=pltpu.HBM)
    dma = pltpu.SemaphoreType.DMA
    n_sends = sum(len(s) for s in block_sends().values()) + 4 * PIECES + 2 + 2 + 7 + 7 + 7
    return pl.pallas_call(
        kernel,
        name="attend_and_convolve",
        out_shape=(pltpu.VMEM((2 * ROWS, D), BF16), pltpu.VMEM((KW, D), F32)),
        in_specs=[hbm] * 6,
        out_specs=(vmem, vmem),
        scratch_shapes=[
            pltpu.VMEM((KW, D), F32),
            pltpu.VMEM((NY, NA, KVROWS, 128), BF16),
            pltpu.VMEM((ROWS, D), BF16),
            pltpu.VMEM((ROWS, D), BF16),
            pltpu.VMEM((HEADS, ROWS, DK), BF16),
            pltpu.VMEM((DK, NA * ROWS), BF16),
            pltpu.VMEM((NA * ROWS, 256), BF16),
            pltpu.VMEM((HEADS, ROWS, 128), F32),
            pltpu.VMEM((HEADS, ROWS, 256), F32),
            pltpu.VMEM((2 * ROWS, D), BF16),
            pltpu.VMEM((D // 128, 2 * ROWS, 128), F32),
            pltpu.VMEM((ROWS, D), F32),
            pltpu.VMEM((ROWS + 16, D), F32),
            pltpu.VMEM((ROWS + 16, D), F32),
            pltpu.VMEM((ROWS + 16, D), F32),
            pltpu.VMEM((2, 2, D), F32),
            pltpu.VMEM((2, 2, D), F32),
            pltpu.VMEM((2, 1, D), F32),
            pltpu.VMEM((2, 1, D), F32),
            pltpu.VMEM((64, 128), F32),
            pltpu.VMEM((8, 8, 128), F32),
            pltpu.VMEM((NZ, 8, 128), F32),
            pltpu.VMEM((NY, 8, 128), F32),
            pltpu.VMEM((64, 128), F32),
            dma((12,)),
            dma((n_sends,)),
            dma((NY, NA)),
            dma((NY, NA)),
            dma((4, PIECES)),
            dma((2,)),
            dma((2,)),
            dma((8,)),
            dma((8,)),
            dma((NZ,)),
            dma((NY,)),
            dma((8,)),
        ],
        compiler_params=pltpu.CompilerParams(
            collective_id=0, has_side_effects=True, vmem_limit_bytes=62 * 2**20
        ),
    )(queries, keys, values, features_fine, rc_state, conv_weight)


def body(queries, keys, values, features_fine, rc_state, conv_weight):
    d_fine, d_weight = run(
        queries[0], keys[0], jnp.swapaxes(values[0], 0, 1), features_fine[0], rc_state[0], conv_weight
    )
    return d_fine[None], d_weight


def solution(mesh):
    split = P("dp", "ctx", None)
    return jax.shard_map(
        body, mesh=mesh, in_specs=(split,) * 5 + (P(),), out_specs=(split, P()), check_vma=False
    )
```

```python
import heapq
import math

import jax
import jax.numpy as jnp
from jax import lax
from jax.experimental import pallas as pl
from jax.experimental.pallas import tpu as pltpu
from jax.sharding import PartitionSpec as P

HEADS = 8
DK = 128
DV = 192
ROWS = 128
D = HEADS * DV
KW = 5
KVROWS = DK + DV
KPART = 112
PIECES = 4
NA, NY = 4, 8
NX, NZ = 4, 8
MESH = pl.DeviceIdType.MESH
F32 = jnp.float32
BF16 = jnp.bfloat16


def block_sends():
    sends = {}
    for za in range(NA):
        cw = 4 - za % 2
        for dy in range(NY):
            behind = (NY - dy) % NY
            v, k = [], []
            if dy == 0:
                if za == 0:
                    v += [("near", ("V", 1, 0)), ("far", ("V", 2, 0))]
                if za == 2:
                    v.append(("near", ("V", 3, 0)))
                v += [("y+", ("V", za, 7)), ("y-", ("V", za, 1))]
            elif behind <= cw:
                if behind < cw:
                    v.append(("y+", ("V", za, dy - 1)))
            elif dy < 7 - cw:
                v.append(("y-", ("V", za, dy + 1)))
            sends[("V", za, dy)] = v
            if za == 0:
                if dy == 0:
                    k += [("y+", ("K", 0, 7)), ("y-", ("K", 0, 1))]
                elif behind < 4:
                    k.append(("y+", ("K", 0, dy - 1)))
                elif dy < 3:
                    k.append(("y-", ("K", 0, dy + 1)))
                k += [("near", ("K", 1, dy)), ("far", ("K", 2, dy))]
            elif za == 2:
                k.append(("near", ("K", 3, dy)))
            sends[("K", za, dy)] = k
    return sends


def arrival_order(sends):
    free = {"y+": 0.0, "y-": 0.0, "near": 0.0, "far": 0.0}
    slow = {"y+": 1.5, "y-": 1.5, "near": 2.0, "far": 4.0}
    cost = {"V": (KVROWS - KPART) * 0.0055, "K": KPART * 0.0055}
    queue = [(0.0, 0, ("V", 0, 0)), (0.0, 1, ("K", 0, 0))]
    order, n = [], 2
    while queue:
        now, _, key = heapq.heappop(queue)
        order.append(key)
        for link, child in sends[key]:
            end = max(now, free[link]) + cost[key[0]] * slow[link]
            free[link] = end
            heapq.heappush(queue, (end + (1.8 if link[0] == "y" else 2.4), n, child))
            n += 1
    return order


def kernel(
    q_ref, k_ref, v_ref, ff_ref, rc_ref, cw_ref, df_ref, dw_ref,
    w_ref, kv, relay, rcin, qs, kx, vx, top, acc, fine, wide, base, ev, od, grd, halo_out, halo_in, edge_out, edge_in,
    part, e_in, z_in, y_in, final,
    local, send_sem, k_sem, v_sem, m_sem, h_recv, e_recv, s_send, s_recv, z_recv, y_recv, f_recv,
):
    dp, ctx = lax.axis_index("dp"), lax.axis_index("ctx")
    a, y = ctx // NY, lax.rem(ctx, NY)
    core, zlo, x = lax.rem(dp, 2), lax.rem(dp // 2, 2), dp // 4
    z = a * 2 + zlo
    count = NA * NY

    def at(a_new, y_new):
        return (dp, lax.rem(a_new, NA) * NY + lax.rem(y_new, NY))

    right, left = (dp, lax.rem(ctx + 1, count)), (dp, lax.rem(ctx + count - 1, count))
    near, far = a + 1 - 2 * lax.rem(a, 2), NA - 1 - a
    rows_of_a = (a, near, far, NA - 1 - near)
    y_mirror = (dp, a * NY + NY - 1 - y)
    peers = {"y+": at(a, y + 1), "y-": at(a, y + NY - 1), "near": at(near, y), "far": at(far, y)}
    other_core = (dp + 1 - 2 * core, ctx)
    e = x * 2 + core
    e_peers = []
    for i in range(1, 8):
        e_new = lax.rem(e + i, 8)
        e_peers.append((e_new // 2 * 4 + zlo * 2 + lax.rem(e_new, 2), ctx))
    z_peers = []
    for i in range(1, NZ):
        z_new = lax.rem(z + i, NZ)
        z_peers.append((x * 4 + lax.rem(z_new, 2) * 2 + core, z_new // 2 * NY + y))
    y_peers = [at(a, y + i) for i in range(1, NY)]
    barrier = pltpu.get_barrier_semaphore()
    greeted = [right, left, y_mirror] + e_peers + z_peers + y_peers
    for peer in greeted:
        pl.semaphore_signal(barrier, inc=1, device_id=peer, device_id_type=MESH)

    own_k = pltpu.make_async_copy(k_ref, kv.at[y, a, pl.ds(0, DK)], local.at[0])
    own_v = pltpu.make_async_copy(v_ref, kv.at[y, a, pl.ds(DK, DV)], local.at[1])
    own_f = pltpu.make_async_copy(ff_ref, fine, local.at[2])
    own_q = [
        pltpu.make_async_copy(q_ref.at[:, pl.ds(h * DK, DK)], qs.at[h], local.at[3 + h]) for h in range(HEADS)
    ]
    own_w = pltpu.make_async_copy(cw_ref, w_ref, local.at[3 + HEADS])
    for copy in [own_k, own_v, own_f] + own_q + [own_w]:
        copy.start()

    started = []

    def push(src, dst, recv_sem, peer):
        copy = pltpu.make_async_remote_copy(
            src, dst, send_sem.at[len(started)], recv_sem, device_id=peer, device_id_type=MESH
        )
        copy.start()
        started.append(copy)

    def landed(ref, sem):
        pltpu.make_async_remote_copy(ref, ref, sem, sem, device_id=other_core, device_id_type=MESH).wait_recv()

    sends = block_sends()
    order = arrival_order(sends)

    def event(key):
        o_a, o_y = rows_of_a[key[1]], lax.rem(y + key[2], NY)
        if key[0] == "K":
            ref, sem = kv.at[o_y, o_a, pl.ds(0, KPART)], k_sem.at[o_y, o_a]
        else:
            ref, sem = kv.at[o_y, o_a, pl.ds(KPART, KVROWS - KPART)], v_sem.at[o_y, o_a]
        if key[1:] != (0, 0):
            landed(ref, sem)
        for link, _ in sends[key]:
            push(ref, ref, sem, peers[link])

    step = ROWS // 2 // PIECES

    def lanes(i):
        one, two = pl.ds(i * step, step), pl.ds(ROWS // 2 + i * step, step)
        return ((one, 0, y_mirror, peers["far"]), (two, 1, peers["far"], y_mirror))

    def reflect(i):
        for rows, way, peer, _ in lanes(i):
            push(rc_ref.at[rows], relay.at[rows], m_sem.at[way, i], peer)

    def reflect_on(i):
        for rows, way, _, peer in lanes(i):
            landed(relay.at[rows], m_sem.at[way, i])
            push(relay.at[rows], rcin.at[rows], m_sem.at[2 + way, i], peer)

    def reflected(i):
        for rows, way, _, _ in lanes(i):
            landed(rcin.at[rows], m_sem.at[2 + way, i])

    def prepare():
        def heads(h, _):
            top[h] = jnp.full((ROWS, 128), -1e30, F32)
            acc[h] = jnp.zeros((ROWS, 256), F32)
            return 0

        lax.fori_loop(0, HEADS, heads, 0)
        vx[:, DV:256] = jnp.ones((NA * ROWS, 64), BF16)

    def gather_keys(dy):
        o_y = lax.rem(y + dy, NY)
        for i in range(NA):
            rows = slice(i * ROWS, (i + 1) * ROWS)
            kx[:, rows] = kv[o_y, i, 0:DK, :].T
            vx[rows, 0:128] = kv[o_y, i, DK : DK + 128, :].T
            vx[rows, 128:192] = kv[o_y, i, DK + 128 : DK + DV, :].T

    factor = DK ** (-0.5) * math.log2(math.e)

    def attend():
        s = jnp.dot(qs[...].reshape(HEADS * ROWS, DK), kx[...], preferred_element_type=F32)
        old = top[...].reshape(HEADS * ROWS, 128)
        new = jnp.maximum(old, jnp.max(s, axis=1, keepdims=True))
        p = jnp.exp2((s - new[:, :1]) * factor).astype(BF16)
        fade = jnp.exp2((old - new) * factor)
        fade = jnp.concatenate([fade, fade], axis=1)
        total = acc[...].reshape(HEADS * ROWS, 256) * fade + jnp.dot(p, vx[...], preferred_element_type=F32)
        acc[...] = total.reshape(HEADS, ROWS, 256)
        top[...] = new.reshape(HEADS, ROWS, 128)

    def widen():
        def chunk(i, _):
            cols = pl.ds(pl.multiple_of(i * 128, 128), 128)
            wide[i] = fine[:, cols].astype(F32)
            ev[8:136, cols] = wide[i, pl.ds(0, ROWS, stride=2), :]
            od[8:136, cols] = wide[i, pl.ds(1, ROWS, stride=2), :]
            return 0

        lax.fori_loop(0, D // 128, chunk, 0)

    def take_halo():
        landed(halo_in.at[0], h_recv.at[0])
        landed(halo_in.at[1], h_recv.at[1])
        inner_left = jnp.where(ctx > 0, 1.0, 0.0)
        inner_right = jnp.where(ctx < count - 1, 1.0, 0.0)
        ev[7:8, :] = halo_in[0, 0:1, :] * inner_left
        od[7:8, :] = halo_in[0, 1:2, :] * inner_left
        ev[136:137, :] = halo_in[1, 0:1, :] * inner_right

    def convolve(low, high):
        def chunk(i, _):
            cols = pl.ds(pl.multiple_of(i * 128, 128), 128)
            w = w_ref[:, cols]
            base[:, cols] = (
                w[0:1] * ev[7:135, cols]
                + w[1:2] * od[7:135, cols]
                + w[2:3] * ev[8:136, cols]
                + w[3:4] * od[8:136, cols]
                + w[4:5] * ev[9:137, cols]
            )
            return 0

        lax.fori_loop(low, high, chunk, 0)

    own_k.wait()
    own_v.wait()
    pl.semaphore_wait(barrier, len(greeted))

    ready, done = [], {}
    out, back = 0, 0
    for n, key in enumerate(order):
        event(key)
        if out < PIECES and n >= 1 + out * 8:
            reflect(out)
            out += 1
        if n == 1:
            own_f.wait()
            halo_out[0] = fine[2 * ROWS - 16 : 2 * ROWS, :].astype(F32)[14:16]
            halo_out[1] = fine[0:16, :].astype(F32)[0:2]
            push(halo_out.at[0], halo_in.at[0], h_recv.at[0], right)
            push(halo_out.at[1], halo_in.at[1], h_recv.at[1], left)
            for copy in own_q + [own_w]:
                copy.wait()
            prepare()
            widen()
        if back < out and n >= 26 + back * 11:
            reflect_on(back)
            back += 1
        if n == 7:
            take_halo()
        if n in (8, 10, 12, 14):
            convolve((n - 8) // 2 * 3, (n - 8) // 2 * 3 + 3)
        done[key[2]] = done.get(key[2], 0) + 1
        if done[key[2]] == 2 * NA:
            ready.append(key[2])
        if ready and (n > len(order) - 2 or (done[key[2]] != 2 * NA)):
            gather_keys(ready.pop(0))
            attend()
    while ready:
        gather_keys(ready.pop(0))
        attend()
    for i in range(back, PIECES):
        reflect_on(i)
    for i in range(PIECES):
        reflected(i)
    row = lax.broadcasted_iota(jnp.int32, (ROWS, ROWS), 0)
    col = lax.broadcasted_iota(jnp.int32, (ROWS, ROWS), 1)
    turn = jnp.where(row + col == ROWS - 1, 1.0, 0.0).astype(BF16)

    part[60:64, :] = jnp.zeros((4, 128), F32)
    shared, given = [], 0
    for j in range(HEADS // 2):
        cols = slice(j * 2 * DV, (j + 1) * 2 * DV)
        one, two = acc[2 * j], acc[2 * j + 1]
        attended = jnp.concatenate(
            [one[:, :DV] / one[:, DV : DV + 1], two[:, :DV] / two[:, DV : DV + 1]], axis=1
        )
        grd[8:136, cols] = base[:, cols] + attended - jnp.dot(turn, rcin[:, cols], preferred_element_type=F32)
        for i in range(3 * j, 3 * j + 3):
            cols = slice(i * 128, (i + 1) * 128)
            g = grd[8:136, cols]
            taps = (ev[7:135, cols], od[7:135, cols], ev[8:136, cols], od[8:136, cols], ev[9:137, cols])
            part[i * KW : (i + 1) * KW, :] = jnp.concatenate(
                [jnp.sum(g * tap, axis=0, keepdims=True) for tap in taps], axis=0
            )
        while given < 8 and (8 * given + 8 <= 15 * (j + 1) or j == 3):
            copy = pltpu.make_async_remote_copy(
                part.at[pl.ds(8 * given, 8)], e_in.at[e], s_send.at[given], s_recv.at[e],
                device_id=(given // 2 * 4 + zlo * 2 + given % 2, ctx), device_id_type=MESH,
            )
            pl.when(e != given)(copy.start)
            shared.append(copy)
            given += 1
    edge_out[0] = grd[135:136, :]
    edge_out[1] = grd[8:9, :]
    push(edge_out.at[0], edge_in.at[0], e_recv.at[0], right)
    push(edge_out.at[1], edge_in.at[1], e_recv.at[1], left)

    def spread(low, high):
        def chunk(i, _):
            cols = pl.ds(pl.multiple_of(i * 128, 128), 128)
            w = w_ref[:, cols]
            before, here, after = grd[7:135, cols], grd[8:136, cols], grd[9:137, cols]
            wide[i, pl.ds(0, ROWS, stride=2), :] = w[0:1] * after + w[2:3] * here + w[4:5] * before
            wide[i, pl.ds(1, ROWS, stride=2), :] = w[1:2] * after + w[3:4] * here
            df_ref[:, cols] = wide[i].astype(BF16)
            return 0

        lax.fori_loop(low, high, chunk, 0)

    e_in[e] = part[pl.ds(pl.multiple_of(8 * e, 8), 8), :]
    for i in range(1, 8):
        slot = lax.rem(e + i, 8)
        landed(e_in.at[slot], s_recv.at[slot])
    z_in[z] = jnp.sum(e_in[...], axis=0)
    for peer in z_peers:
        push(z_in.at[z], z_in.at[z], z_recv.at[z], peer)
    landed(edge_in.at[0], e_recv.at[0])
    landed(edge_in.at[1], e_recv.at[1])
    grd[7:8, :] = edge_in[0] * jnp.where(ctx > 0, 1.0, 0.0)
    grd[136:137, :] = edge_in[1] * jnp.where(ctx < count - 1, 1.0, 0.0)
    spread(0, 6)
    for i in range(1, NZ):
        slot = lax.rem(z + i, NZ)
        landed(z_in.at[slot], z_recv.at[slot])
    y_in[y] = jnp.sum(z_in[...], axis=0)
    for peer in y_peers:
        push(y_in.at[y], y_in.at[y], y_recv.at[y], peer)
    spread(6, 12)
    for i in range(1, NY):
        slot = lax.rem(y + i, NY)
        landed(y_in.at[slot], y_recv.at[slot])
    final[pl.ds(pl.multiple_of(8 * e, 8), 8), :] = jnp.sum(y_in[...], axis=0) * (1.0 / math.sqrt(NX * 4 * count * ROWS))
    mine = final.at[pl.ds(pl.multiple_of(8 * e, 8), 8)]
    for peer in e_peers:
        push(mine, mine, f_recv.at[e], peer)
    for i in range(1, 8):
        slot = lax.rem(e + i, 8)
        landed(final.at[pl.ds(pl.multiple_of(8 * slot, 8), 8)], f_recv.at[slot])
    for i in range(D // 128):
        dw_ref[:, i * 128 : (i + 1) * 128] = final[i * KW : (i + 1) * KW, :]
    for i, copy in enumerate(shared):
        pl.when(e != i)(copy.wait_send)
    for copy in started:
        copy.wait_send()


def run(queries, keys, values, features_fine, rc_state, conv_weight):
    vmem, hbm = pl.BlockSpec(memory_space=pltpu.VMEM), pl.BlockSpec(memory_space=pltpu.HBM)
    dma = pltpu.SemaphoreType.DMA
    n_sends = sum(len(s) for s in block_sends().values()) + 4 * PIECES + 2 + 2 + 7 + 7 + 7
    return pl.pallas_call(
        kernel,
        name="attend_and_convolve",
        out_shape=(pltpu.VMEM((2 * ROWS, D), BF16), pltpu.VMEM((KW, D), F32)),
        in_specs=[hbm] * 6,
        out_specs=(vmem, vmem),
        scratch_shapes=[
            pltpu.VMEM((KW, D), F32),
            pltpu.VMEM((NY, NA, KVROWS, 128), BF16),
            pltpu.VMEM((ROWS, D), BF16),
            pltpu.VMEM((ROWS, D), BF16),
            pltpu.VMEM((HEADS, ROWS, DK), BF16),
            pltpu.VMEM((DK, NA * ROWS), BF16),
            pltpu.VMEM((NA * ROWS, 256), BF16),
            pltpu.VMEM((HEADS, ROWS, 128), F32),
            pltpu.VMEM((HEADS, ROWS, 256), F32),
            pltpu.VMEM((2 * ROWS, D), BF16),
            pltpu.VMEM((D // 128, 2 * ROWS, 128), F32),
            pltpu.VMEM((ROWS, D), F32),
            pltpu.VMEM((ROWS + 16, D), F32),
            pltpu.VMEM((ROWS + 16, D), F32),
            pltpu.VMEM((ROWS + 16, D), F32),
            pltpu.VMEM((2, 2, D), F32),
            pltpu.VMEM((2, 2, D), F32),
            pltpu.VMEM((2, 1, D), F32),
            pltpu.VMEM((2, 1, D), F32),
            pltpu.VMEM((64, 128), F32),
            pltpu.VMEM((8, 8, 128), F32),
            pltpu.VMEM((NZ, 8, 128), F32),
            pltpu.VMEM((NY, 8, 128), F32),
            pltpu.VMEM((64, 128), F32),
            dma((12,)),
            dma((n_sends,)),
            dma((NY, NA)),
            dma((NY, NA)),
            dma((4, PIECES)),
            dma((2,)),
            dma((2,)),
            dma((8,)),
            dma((8,)),
            dma((NZ,)),
            dma((NY,)),
            dma((8,)),
        ],
        compiler_params=pltpu.CompilerParams(
            collective_id=0, has_side_effects=True, vmem_limit_bytes=62 * 2**20
        ),
    )(queries, keys, values, features_fine, rc_state, conv_weight)


def body(queries, keys, values, features_fine, rc_state, conv_weight):
    d_fine, d_weight = run(
        queries[0], keys[0], jnp.swapaxes(values[0], 0, 1), features_fine[0], rc_state[0], conv_weight
    )
    return d_fine[None], d_weight


def solution(mesh):
    split = P("dp", "ctx", None)
    return jax.shard_map(
        body, mesh=mesh, in_specs=(split,) * 5 + (P(),), out_specs=(split, P()), check_vma=False
    )
```
